32 devices in a mesh: dp: 4 (over z), blk: 8 (over y, x, core).
Axes of the slice: x: 2, y: 2, z: 4, core: 2. Of those that a mesh axis runs over, the one named last changes fastest.
Arguments:
- tokens: bfloat16 [8192, 1152], P(('dp', 'blk')), may hold values from -6 to 6
- cond: bfloat16 [20, 1152], replicated, may hold values from -6 to 6
- segments: int32 [8192], P(('dp', 'blk')), may hold values from 0 to 19, as said below
- kept: int32 [4096], P(('dp', 'blk')), may hold values from 0 to 255, as said below
- cotangent: bfloat16 [8192, 1152], P(('dp', 'blk')), may hold values from -6 to 6
- ada_weight: bfloat16 [2, 1152, 6912], P(None, 'dp'), may hold values from -0.1875 to 0.1875
- ada_bias: bfloat16 [2, 6912], P(None, 'dp'), may hold values from -3 to 3
- qkv_weight: bfloat16 [2, 1152, 3456], P(None, 'dp'), may hold values from -0.1875 to 0.1875
- qv_bias: bfloat16 [2, 2304], P(None, 'dp'), may hold values from -3 to 3
- out_weight: bfloat16 [2, 1152, 1152], P(None, 'dp'), may hold values from -2 to 2
- out_bias: bfloat16 [2, 1152], P(None, 'dp'), may hold values from -3 to 3
- up_weight: bfloat16 [2, 1152, 4608], P(None, 'dp'), may hold values from -0.1875 to 0.1875
- up_bias: bfloat16 [2, 4608], P(None, 'dp'), may hold values from -3 to 3
- down_weight: bfloat16 [2, 4608, 1152], P(None, 'dp'), may hold values from -0.09375 to 0.09375
- down_bias: bfloat16 [2, 1152], P(None, 'dp'), may hold values from -3 to 3
Outputs:
- mid: float32 [8192, 1152], P(('dp', 'blk'))
- final: float32 [8192, 1152], P(('dp', 'blk'))
- grad_tokens: float32 [8192, 1152], P(('dp', 'blk'))
- grad_ada_weight: float32 [2, 1152, 6912], P(None, 'dp')
- grad_ada_bias: float32 [2, 6912], P(None, 'dp')
- grad_qkv_weight: float32 [2, 1152, 3456], P(None, 'dp')
- grad_qv_bias: float32 [2, 2304], P(None, 'dp')
- grad_out_weight: float32 [2, 1152, 1152], P(None, 'dp')
- grad_out_bias: float32 [2, 1152], P(None, 'dp')
- grad_up_weight: float32 [2, 1152, 4608], P(None, 'dp')
- grad_up_bias: float32 [2, 4608], P(None, 'dp')
- grad_down_weight: float32 [2, 4608, 1152], P(None, 'dp')
- grad_down_bias: float32 [2, 1152], P(None, 'dp')
The draws below stay inside these ranges and needn't reach their ends.
Inputs may be any that keep to these rules, and one draw needn't show every extreme that they name: `segments`: each block of 2048 consecutive tokens (one index of dp, number g) holds images g * 5 to g * 5 + 4: first 1 images of 1024 tokens, then 4 of 256. Every device's 256 rows hold the same number of tokens of each image of its block, in a random order. `kept`: for each device in turn, 128 distinct numbers of its own rows, increasing: the tokens that pass through the second block.
All inputs are finite; a program needn't handle non-finite values.
Results may differ from the reference program's by a relative error of at most 0.025.
Values may be sent and summed in bfloat16 or wider, within the bound.
No kernel may reach another device: no remote copies, remote signals or barrier semaphores. Data moves between devices by JAX's collectives and lax.ppermute only.
A program may use at most 448 MiB of HBM per device.

```python
from functools import partial
import jax
import jax.numpy as jnp
from jax import lax

HEADS = 16
HEAD_DIM = 72
FF = 4608
TOK_DEV = 256
BIG_LEN = 1024
SMALL_LEN = 256
BLOCKS = 2
D = 1152
KEEP = 128
BIG_IMG = 1
SMALL_IMG = 4
IMG_GROUP = 5
IMAGES = 20
TOKENS = 8192
N_DP = 4
N_BLK = 8


def draw_segments(key, part):
    key = jax.random.fold_in(key, 11)
    per_big = BIG_LEN // N_BLK
    per_small = SMALL_LEN // N_BLK
    row_ids = jnp.concatenate([jnp.repeat(jnp.arange(BIG_IMG, dtype=jnp.int32), per_big), BIG_IMG + jnp.repeat(jnp.arange(SMALL_IMG, dtype=jnp.int32), per_small)])
    key_list = jax.random.split(key, N_DP * N_BLK)

    def shuffle_rows(sub_key):
        return jax.random.permutation(sub_key, row_ids)
    shuffled = jax.vmap(shuffle_rows)(key_list)
    offsets = jnp.arange(N_DP * N_BLK, dtype=jnp.int32) // N_BLK * IMG_GROUP
    return (shuffled + offsets[:, None]).reshape(-1).astype(jnp.int32)


def draw_kept(key, part):
    key = jax.random.fold_in(key, 23)
    key_list = jax.random.split(key, N_DP * N_BLK)

    def choose_rows(sub_key):
        return jnp.sort(jax.random.permutation(sub_key, TOK_DEV)[:KEEP])
    return jax.vmap(choose_rows)(key_list).reshape(-1).astype(jnp.int32)


def block_levels(stream_key, extent, cuts, least, top_value):
    gain = 1.0
    for dim, parts in cuts:
        heights = jax.random.uniform(jax.random.fold_in(jax.random.fold_in(stream_key, 6), dim), (parts,), jnp.float32, least / len(cuts), top_value / len(cuts))
        gain = gain * jnp.repeat(jnp.exp(heights), extent[dim] // parts).reshape((-1,) + (1,) * (len(extent) - 1 - dim))
    return gain


def centred(own_key, shape, width, reach, cuts=(), kind=jnp.bfloat16):
    values = jax.random.normal(own_key, shape, jnp.float32) * width
    if len(cuts) > 0:
        values = block_levels(own_key, shape, cuts, -0.22, 0.18) * values
    return jnp.clip(values, min=-reach, max=reach).astype(kind)


def setup_inputs(seed: int = 0) -> dict:
    arg_keys = jax.random.split(jax.random.key(seed), 16)
    tokens = centred(arg_keys[0], (TOKENS, D), 1.0, 6.0, ((0, 32),))
    cond = centred(arg_keys[1], (IMAGES, D), 1.0, 6.0)
    segments = draw_segments(jax.random.fold_in(arg_keys[15], 71), 0)
    kept = draw_kept(jax.random.fold_in(arg_keys[15], 71), 0)
    cotangent = centred(arg_keys[4], (TOKENS, D), 1.0, 6.0, ((0, 32),))
    ada_weight = centred(arg_keys[5], (BLOCKS, D, 6 * D), D ** -0.5, 0.1875, ((1, 4),))
    ada_bias = centred(arg_keys[6], (BLOCKS, 6 * D), 0.5, 3.0, ((1, 4),))
    qkv_weight = centred(arg_keys[7], (BLOCKS, D, 3 * D), D ** -0.5, 0.1875, ((1, 4),))
    qv_bias = centred(arg_keys[8], (BLOCKS, 2 * D), 0.5, 3.0, ((1, 4),))
    out_weight = centred(arg_keys[9], (BLOCKS, D, D), (HEAD_DIM // 8) ** -0.5, 2.0, ((1, 4),))
    out_bias = centred(arg_keys[10], (BLOCKS, D), 0.5, 3.0, ((1, 4),))
    up_weight = centred(arg_keys[11], (BLOCKS, D, FF), D ** -0.5, 0.1875, ((1, 4),))
    up_bias = centred(arg_keys[12], (BLOCKS, FF), 0.5, 3.0, ((1, 4),))
    down_weight = centred(arg_keys[13], (BLOCKS, FF, D), FF ** -0.5, 0.09375, ((1, 4),))
    down_bias = centred(arg_keys[14], (BLOCKS, D), 0.5, 3.0, ((1, 4),))
    return {"tokens": tokens, "cond": cond, "segments": segments, "kept": kept, "cotangent": cotangent, "ada_weight": ada_weight, "ada_bias": ada_bias, "qkv_weight": qkv_weight, "qv_bias": qv_bias, "out_weight": out_weight, "out_bias": out_bias, "up_weight": up_weight, "up_bias": up_bias, "down_weight": down_weight, "down_bias": down_bias}


@jax.custom_vjp
def low(v):
    return lax.optimization_barrier(v.astype(jnp.bfloat16)).astype(jnp.float32)

@jax.custom_vjp
def low_back(v):
    return v

def low_keep(v):
    return (low(v), None)

def low_pass(kept, grad):
    return (grad,)

def back_keep(v):
    return (v, None)

def back_low(kept, grad):
    return (low(grad),)
low.defvjp(low_keep, low_pass)
low_back.defvjp(back_keep, back_low)
epsilon = 1e-06
highest = lax.Precision.HIGHEST

def product(left, right):
    return jnp.dot(left, right, precision=highest, preferred_element_type=jnp.float32)

def norm_rows(values):
    centered = values - lax.optimization_barrier(jnp.mean(values, axis=-1, keepdims=True))
    return centered * lax.rsqrt(lax.optimization_barrier(jnp.mean(centered * centered, axis=-1, keepdims=True)) + epsilon)

def query_block(key_heads, value_heads, key_seg, query_heads, query_seg):
    raw_scores = jnp.einsum('qhd,khd->hqk', query_heads, key_heads, precision=highest)
    scores = low_back(raw_scores) * HEAD_DIM ** (-0.5)
    same_image = query_seg[None, :, None] == key_seg[None, None, :]
    weights = jnp.where(same_image, jnp.exp(jnp.where(same_image, scores, 0.0)), 0.0)
    totals = lax.optimization_barrier(jnp.sum(weights, axis=-1))
    summed = low_back(jnp.einsum('hqk,khd->qhd', low(weights), value_heads, precision=highest))
    return (summed / jnp.transpose(totals)[:, :, None]).reshape(query_heads.shape[0], -1)

def attend_group(group):
    queries, key_rows, values, group_seg = group
    row_count = queries.shape[0]
    block_rows = min(512, row_count)
    key_heads = key_rows.reshape(row_count, HEADS, HEAD_DIM)
    value_heads = values.reshape(row_count, HEADS, HEAD_DIM)
    one_block = jax.checkpoint(partial(query_block, key_heads, value_heads, group_seg))
    query_blocks = queries.reshape(row_count // block_rows, block_rows, HEADS, HEAD_DIM)
    seg_blocks = group_seg.reshape(row_count // block_rows, block_rows)
    outputs = lax.map(lambda item_pair: one_block(item_pair[0], item_pair[1]), (query_blocks, seg_blocks))
    return outputs.reshape(row_count, HEADS * HEAD_DIM)

def by_group(array):
    return array.reshape((N_DP, -1) + array.shape[1:])

def attention(queries, key_rows, values, seg_rows):
    outputs = lax.map(attend_group, (by_group(queries), by_group(key_rows), by_group(values), by_group(seg_rows)))
    return outputs.reshape(queries.shape)

def block(layer_index, residual, seg_rows, params, silu_cond):
    ada_weight, ada_bias, qkv_weight, qv_bias, out_weight, out_bias, up_weight, up_bias, down_weight, down_bias = params
    modulation = product(silu_cond, ada_weight[layer_index]) + ada_bias[layer_index]
    per_token = jnp.take(modulation, seg_rows, axis=0)
    shift_one, scale_one, gate_one, shift_two, scale_two, gate_two = jnp.split(per_token, 6, axis=1)
    first_in = low(norm_rows(residual) * (1.0 + scale_one) + shift_one)
    joined = product(first_in, qkv_weight[layer_index])
    queries = low(low_back(joined[:, :D] + qv_bias[layer_index, :D]))
    key_rows = low(low_back(joined[:, D:2 * D]))
    values = low(low_back(joined[:, 2 * D:] + qv_bias[layer_index, D:]))
    attended = attention(queries, key_rows, values, seg_rows)
    mixed_rows = low(low_back(attended))
    branch = low_back(product(mixed_rows, out_weight[layer_index]) + out_bias[layer_index])
    middle = residual + gate_one * branch
    second = low(norm_rows(middle) * (1.0 + scale_two) + shift_two)
    hidden = low_back(product(second, up_weight[layer_index]) + up_bias[layer_index])
    active = low(jax.nn.gelu(hidden, approximate=True))
    output = low_back(product(active, down_weight[layer_index]) + down_bias[layer_index])
    return middle + gate_two * output

def reference(tokens, cond, segments, kept, cotangent, ada_weight, ada_bias, qkv_weight, qv_bias, out_weight, out_bias, up_weight, up_bias, down_weight, down_bias):
    keep_rows = jnp.arange(kept.shape[0], dtype=jnp.int32) // KEEP * TOK_DEV + kept.astype(jnp.int32)

    def forward(residual, cond_rows, *params):
        silu_cond = low(jax.nn.silu(cond_rows))
        middle_out = block(0, residual, segments, params, silu_cond)
        routed = block(1, middle_out[keep_rows], segments[keep_rows], params, silu_cond)
        return (middle_out, middle_out.at[keep_rows].set(routed))
    floats = tuple((array.astype(jnp.float32) for array in (tokens, cond, ada_weight, ada_bias, qkv_weight, qv_bias, out_weight, out_bias, up_weight, up_bias, down_weight, down_bias)))
    outputs, pull = jax.vjp(forward, *floats)
    mid, final = outputs
    grads = pull((jnp.zeros_like(mid), cotangent.astype(jnp.float32)))
    return (mid, final, grads[0], grads[2], grads[3], grads[4], grads[5], grads[6], grads[7], grads[8], grads[9], grads[10], grads[11])
```

```python
import functools
import math

import jax
import jax.numpy as jnp
from jax import lax
from jax.experimental import pallas as pl
from jax.experimental.pallas import tpu as pltpu
from jax.sharding import PartitionSpec as P

HEADS = 16
BIG_LEN = 1024
SMALL_LEN = 256
PAD = 128
epsilon = 1e-06
highest = lax.Precision.HIGHEST
bf16 = jnp.bfloat16
f32 = jnp.float32
VMEM_LIMIT = 56 * 1024 * 1024

NN = (((1,), (0,)), ((), ()))
NT = (((1,), (1,)), ((), ()))
TN = (((0,), (0,)), ((), ()))


def dot(left, right, dims=NN):
    return lax.dot_general(left, right, dims, preferred_element_type=f32)


def swap(x, bit, n):
    return lax.ppermute(x, "blk", [(i, i ^ bit) for i in range(n)])


def gather_rows(x, n):
    if n == 8:
        rows = x.shape[0]
        half = rows // 2
        c1 = swap(x, 1, n)
        x2 = swap(x, 2, n)
        x4 = swap(x, 4, n)
        d0 = swap(x4[:half], 2, n)
        d1 = swap(x2[half:], 4, n)
        x3 = swap(x2, 1, n)
        x5 = swap(x4, 1, n)
        e0 = swap(d0, 1, n)
        e1 = swap(d1, 1, n)
        return [
            (x, 0, 0),
            (c1, 1, 0),
            (x2, 2, 0),
            (x3, 3, 0),
            (x4, 4, 0),
            (x5, 5, 0),
            (d0, 6, 0),
            (d1, 6, half),
            (e0, 7, 0),
            (e1, 7, half),
        ]
    pieces = {0: x}
    bit = n // 2
    while bit:
        for k in list(pieces):
            pieces[k | bit] = swap(pieces[k], bit, n)
        bit //= 2
    return [(pieces[k], k, 0) for k in sorted(pieces)]


def reduce_rows(even, odd, n):
    got = swap(odd, 1, n)
    total = even.astype(f32) + got.astype(f32)
    if n == 8:
        half = total.shape[1] // 2
        q0, q1, q2, q3 = (total[j] for j in range(4))
        s3 = q3.astype(bf16)
        a0 = swap(s3[:half], 2, n)
        a1 = swap(s3[half:], 4, n)
        r1a = swap(q1[:half].astype(bf16), 2, n)
        r2b = swap(q2[half:].astype(bf16), 4, n)
        r1b = swap((q1[half:] + a1.astype(f32)).astype(bf16), 2, n)
        r2a = swap((q2[:half] + a0.astype(f32)).astype(bf16), 4, n)
        top = q0[:half] + r1a.astype(f32) + r2a.astype(f32)
        low = q0[half:] + r1b.astype(f32) + r2b.astype(f32)
        return jnp.concatenate([top, low], axis=0)
    bit = n // 2
    while bit > 1:
        step = bit // 2
        got = swap(total[step:].astype(bf16), bit, n)
        total = total[:step] + got.astype(f32)
        bit //= 2
    return total[0]


def load_chunks(chunks, refs, held, sems):
    copies = []
    for i, (k, off, rows) in enumerate(chunks):
        copies.append(pltpu.make_async_copy(refs[i], held.at[k, pl.ds(off, rows)], sems.at[i]))
    for copy in copies:
        copy.start()
    for copy in copies:
        copy.wait()


def chunk_plan(chunks):
    return tuple((k, off, array.shape[0]) for array, k, off in chunks)


def call(kernel, name, chunks, args, outs, scratch, flops):
    arrays = [c[0] for c in chunks]
    moved = sum(a.size * a.dtype.itemsize for a in arrays + list(args))
    moved += sum(math.prod(o.shape) * o.dtype.itemsize for o in outs)
    sems = [pltpu.SemaphoreType.DMA((max(1, len(arrays)),))]
    vmem = pl.BlockSpec(memory_space=pltpu.VMEM)
    return pl.pallas_call(
        kernel,
        name=name,
        out_shape=outs,
        in_specs=[pl.BlockSpec(memory_space=pl.ANY)] * len(arrays) + [vmem] * len(args),
        out_specs=[vmem] * len(outs),
        scratch_shapes=scratch + sems,
        compiler_params=pltpu.CompilerParams(vmem_limit_bytes=VMEM_LIMIT),
        cost_estimate=pl.CostEstimate(flops=flops, bytes_accessed=moved, transcendentals=0),
    )(*arrays, *args)


def sds(shape, dtype):
    return jax.ShapeDtypeStruct(shape, dtype)


def attn_forward_kernel(plan, images, masked, scale, nh, *refs):
    count = len(plan)
    chunk_refs, refs = refs[:count], refs[count:]
    wqkv, bias, wout = refs[:3]
    refs = refs[3:]
    if masked:
        seg_col, seg_row = refs[:2]
        refs = refs[2:]
    qkv, al, mixed, even, odd, held, rowmix, sems = refs
    n, rows, feats = held.shape
    parts = 3 * nh
    hd = wout.shape[0] // nh
    load_chunks(plan, chunk_refs, held, sems)

    @pl.loop(0, n)
    def _(k):
        proj = (dot(held[k], wqkv[...]) + bias[...]).astype(bf16)
        for p in range(parts):
            part = proj[:, p * PAD : (p + 1) * PAD]
            for off, size, base in images:
                qkv[p, pl.ds(base + k * size, size), :] = part[off : off + size]

    lane = lax.broadcasted_iota(jnp.int32, (1, PAD), 1)
    for off, size, base in images:
        length = size * n
        tile = min(256, length)

        @pl.loop(0, nh * (length // tile))
        def _(step):
            h = step // (length // tile)
            start = base + (step % (length // tile)) * tile
            q = qkv[h, pl.ds(start, tile), :]
            keys = qkv[nh + h, pl.ds(base, length), :]
            vals = qkv[2 * nh + h, pl.ds(base, length), :]
            e = jnp.exp2(dot(q, keys, NT) * (scale * math.log2(math.e)))
            if masked:
                e = jnp.where(seg_col[pl.ds(start, tile), :] == seg_row[...], e, 0.0)
            acc = dot(e.astype(bf16), vals)
            l = acc[:, PAD_L : PAD_L + 1]
            attn = acc / l
            al[h, pl.ds(start, tile), :] = jnp.where(lane == PAD_L, l, attn)
            rowmix[h, pl.ds(start, tile), :] = attn.astype(bf16)

    @pl.loop(0, n // 2)
    def _(j):
        for side, out in ((0, even), (1, odd)):
            k = 2 * j + side
            for off, size, base in images:
                for h in range(nh):
                    mixed[k, pl.ds(off, size), h * PAD : (h + 1) * PAD] = rowmix[
                        h, pl.ds(base + k * size, size), :
                    ]
            out[j] = dot(mixed[k], wout[...]).astype(bf16)


PAD_L = 72


def attn_forward(chunks, wqkv, bias, wout, segs, n, images, scale, nh):
    rows = sum(size for _, size, _ in images)
    total = rows * n
    feats = wqkv.shape[0]
    masked = segs is not None
    outs = [
        sds((3 * nh, total, PAD), bf16),
        sds((nh, total, PAD), f32),
        sds((n, rows, nh * PAD), bf16),
        sds((n // 2, rows, feats), bf16),
        sds((n // 2, rows, feats), bf16),
    ]
    scratch = [pltpu.VMEM((n, rows, feats), bf16), pltpu.VMEM((nh, total, PAD), bf16)]
    flops = 2 * total * feats * 4 * nh * PAD + 4 * nh * total * total * PAD
    return call(
        functools.partial(attn_forward_kernel, chunk_plan(chunks), images, masked, scale, nh),
        "attn_forward",
        chunks,
        [wqkv, bias, wout] + (list(segs) if masked else []),
        outs,
        scratch,
        flops,
    )


def attn_backward_kernel(plan, images, masked, scale, nh, *refs):
    count = len(plan)
    chunk_refs, refs = refs[:count], refs[count:]
    wqkv, wout, qkv, al = refs[:4]
    refs = refs[4:]
    if masked:
        seg_col, seg_row = refs[:2]
        refs = refs[2:]
    dqkv, sums, even, odd, held, gext, grads, dqt, sems = refs
    n, rows, feats = held.shape
    parts = 3 * nh
    load_chunks(plan, chunk_refs, held, sems)
    lane = lax.broadcasted_iota(jnp.int32, (1, PAD), 1)

    @pl.loop(0, n)
    def _(k):
        d_all = dot(held[k], wout[...], NT).astype(bf16).astype(f32)
        for h in range(nh):
            d_head = d_all[:, h * PAD : (h + 1) * PAD]
            for off, size, base in images:
                here = pl.ds(base + k * size, size)
                known = al[h, here, :]
                d = d_head[off : off + size]
                inverse = 1.0 / known[:, PAD_L : PAD_L + 1]
                dotted = jnp.where(lane < PAD_L, d * known, 0.0)
                minus = -jnp.sum(dotted, axis=1, keepdims=True) * inverse
                top = minus.astype(bf16).astype(f32)
                ext = jnp.where(lane == PAD_L, top, jnp.where(lane == PAD_L + 1, minus - top, 0.0))
                gext[h, here, :] = jnp.where(lane < PAD_L, d * inverse, ext).astype(bf16)

    for off, size, base in images:
        length = size * n
        tile = min(256, length)

        @pl.loop(0, nh)
        def _(h):
            queries = qkv[h, pl.ds(base, length), :]
            carried = gext[h, pl.ds(base, length), :]

            @pl.loop(0, length // tile)
            def _(t):
                here = pl.ds(base + t * tile, tile)
                keys = qkv[nh + h, here, :]
                vals = qkv[2 * nh + h, here, :]
                e = jnp.exp2(dot(keys, queries, NT) * (scale * math.log2(math.e)))
                if masked:
                    e = jnp.where(seg_col[here, :] == seg_row[...], e, 0.0)
                er = e.astype(bf16)
                raw = (e * dot(vals, carried, NT)).astype(bf16)
                dv = jnp.where(lane < PAD_L, dot(er, carried), 0.0)
                grads[2 * nh + h, here, :] = dv.astype(bf16)
                grads[nh + h, here, :] = (dot(raw, queries) * scale).astype(bf16)
                added = dot(keys.T, raw)

                @pl.when(t == 0)
                def _():
                    dqt[:, :length] = added

                @pl.when(t > 0)
                def _():
                    dqt[:, :length] += added

            grads[h, pl.ds(base, length), :] = (dqt[:, :length].T * scale).astype(bf16)

    sums[...] = jnp.zeros_like(sums)

    @pl.loop(0, n // 2)
    def _(j):
        for side, out in ((0, even), (1, odd)):
            k = 2 * j + side
            for off, size, base in images:
                for p in range(parts):
                    dqkv[k, pl.ds(off, size), p * PAD : (p + 1) * PAD] = grads[
                        p, pl.ds(base + k * size, size), :
                    ]
            block = dqkv[k]
            sums[...] += jnp.sum(block.astype(f32), axis=0, keepdims=True)
            out[j] = dot(block, wqkv[...], NT).astype(bf16)


def attn_backward(chunks, wqkv, wout, qkv, al, segs, n, images, scale, nh):
    rows = sum(size for _, size, _ in images)
    total = rows * n
    feats = wqkv.shape[0]
    masked = segs is not None
    longest = max(size for _, size, _ in images) * n
    outs = [
        sds((n, rows, 3 * nh * PAD), bf16),
        sds((1, 3 * nh * PAD), f32),
        sds((n // 2, rows, feats), bf16),
        sds((n // 2, rows, feats), bf16),
    ]
    scratch = [
        pltpu.VMEM((n, rows, feats), bf16),
        pltpu.VMEM((nh, total, PAD), bf16),
        pltpu.VMEM((3 * nh, total, PAD), bf16),
        pltpu.VMEM((PAD, longest), f32),
    ]
    flops = 2 * total * feats * 4 * nh * PAD + 10 * nh * total * total * PAD
    return call(
        functools.partial(attn_backward_kernel, chunk_plan(chunks), images, masked, scale, nh),
        "attn_backward",
        chunks,
        [wqkv, wout, qkv, al] + (list(segs) if masked else []),
        outs,
        scratch,
        flops,
    )


def attn_weights_kernel(plan_first, plan_back, *refs):
    a, b = len(plan_first), len(plan_back)
    first_refs, back_refs, refs = refs[:a], refs[a : a + b], refs[a + b :]
    dqkv, mixed, spread, g_qkv, g_out, sums, held, wide, sems = refs
    n, rows, feats = held.shape
    load_chunks(plan_first, first_refs, held, sems)
    left = held[...].reshape(n * rows, feats)
    right = dqkv[...].reshape(n * rows, dqkv.shape[2])
    wide[...] = dot(left, right, TN).astype(bf16)
    g_qkv[...] = dot(wide[...], spread[...], NT).astype(bf16)
    load_chunks(plan_back, back_refs, held, sems)
    back = held[...].reshape(n * rows, feats)
    sums[...] = jnp.sum(back.astype(f32), axis=0, keepdims=True)
    left = mixed[...].reshape(n * rows, mixed.shape[2])
    tall = dot(left, back, TN).astype(bf16)
    width, wider = g_out.shape[0], tall.shape[0]
    g_out[...] = dot(spread[:width, :wider], tall).astype(bf16)


def attn_weights(first_chunks, back_chunks, dqkv, mixed, spread, nh, hd):
    n, rows, _ = dqkv.shape
    feats = first_chunks[0][0].shape[1]
    outs = [sds((feats, 3 * nh * hd), bf16), sds((nh * hd, feats), bf16), sds((1, feats), f32)]
    scratch = [
        pltpu.VMEM((n, rows, feats), bf16),
        pltpu.VMEM((feats, dqkv.shape[2]), bf16),
    ]
    return call(
        functools.partial(attn_weights_kernel, chunk_plan(first_chunks), chunk_plan(back_chunks)),
        "attn_weights",
        first_chunks + back_chunks,
        [dqkv, mixed, spread],
        outs,
        scratch,
        2 * n * rows * feats * 4 * nh * PAD,
    )


def gelu_and_slope(u):
    c = math.sqrt(2.0 / math.pi)
    square = u * u
    t = jnp.tanh(c * u * (1.0 + 0.044715 * square))
    half = 0.5 * (1.0 + t)
    slope = half + 0.5 * u * (1.0 - t * t) * (c * (1.0 + 3.0 * 0.044715 * square))
    return u * half, slope


def mlp_forward_kernel(plan, *refs):
    count = len(plan)
    chunk_refs, refs = refs[:count], refs[count:]
    wup, bias, wdown, active, slope, even, odd, held, sems = refs
    n = held.shape[0]
    load_chunks(plan, chunk_refs, held, sems)

    @pl.loop(0, n // 2)
    def _(j):
        for side, out in ((0, even), (1, odd)):
            k = 2 * j + side
            act, slp = gelu_and_slope(dot(held[k], wup[...]) + bias[...])
            act = act.astype(bf16)
            active[k] = act
            slope[k] = slp.astype(bf16)
            out[j] = dot(act, wdown[...]).astype(bf16)


def mlp_forward(chunks, wup, bias, wdown, n):
    rows, feats = chunks[0][0].shape
    hidden = wup.shape[1]
    outs = [
        sds((n, rows, hidden), bf16),
        sds((n, rows, hidden), bf16),
        sds((n // 2, rows, feats), bf16),
        sds((n // 2, rows, feats), bf16),
    ]
    return call(
        functools.partial(mlp_forward_kernel, chunk_plan(chunks)),
        "mlp_forward",
        chunks,
        [wup, bias, wdown],
        outs,
        [pltpu.VMEM((n, rows, feats), bf16)],
        4 * n * rows * feats * hidden,
    )


def mlp_backward_kernel(plan, *refs):
    count = len(plan)
    chunk_refs, refs = refs[:count], refs[count:]
    wup, wdown, slope, back, even, odd, held, sems = refs
    n = held.shape[0]
    load_chunks(plan, chunk_refs, held, sems)

    @pl.loop(0, n // 2)
    def _(j):
        for side, out in ((0, even), (1, odd)):
            k = 2 * j + side
            grad = (dot(held[k], wdown[...], NT) * slope[k].astype(f32)).astype(bf16)
            back[k] = grad
            out[j] = dot(grad, wup[...], NT).astype(bf16)


def mlp_backward(chunks, wup, wdown, slope):
    n, rows, hidden = slope.shape
    feats = wup.shape[0]
    outs = [
        sds((n, rows, hidden), bf16),
        sds((n // 2, rows, feats), bf16),
        sds((n // 2, rows, feats), bf16),
    ]
    return call(
        functools.partial(mlp_backward_kernel, chunk_plan(chunks)),
        "mlp_backward",
        chunks,
        [wup, wdown, slope],
        outs,
        [pltpu.VMEM((n, rows, feats), bf16)],
        4 * n * rows * feats * hidden,
    )


def mlp_weights_kernel(plan_second, plan_out, *refs):
    a, b = len(plan_second), len(plan_out)
    second_refs, out_refs, refs = refs[:a], refs[a : a + b], refs[a + b :]
    active, back, g_up, g_down, s_up, s_down, held, sems = refs
    n, rows, feats = held.shape
    hidden = active.shape[2]
    load_chunks(plan_second, second_refs, held, sems)
    back_rows = back[...].reshape(n * rows, hidden)
    s_up[...] = jnp.sum(back_rows.astype(f32), axis=0, keepdims=True)
    g_up[...] = dot(held[...].reshape(n * rows, feats), back_rows, TN).astype(bf16)
    load_chunks(plan_out, out_refs, held, sems)
    out_rows = held[...].reshape(n * rows, feats)
    s_down[...] = jnp.sum(out_rows.astype(f32), axis=0, keepdims=True)
    g_down[...] = dot(active[...].reshape(n * rows, hidden), out_rows, TN).astype(bf16)


def mlp_weights(second_chunks, out_chunks, active, back):
    n, rows, hidden = active.shape
    feats = second_chunks[0][0].shape[1]
    outs = [
        sds((feats, hidden), bf16),
        sds((hidden, feats), bf16),
        sds((1, hidden), f32),
        sds((1, feats), f32),
    ]
    return call(
        functools.partial(mlp_weights_kernel, chunk_plan(second_chunks), chunk_plan(out_chunks)),
        "mlp_weights",
        second_chunks + out_chunks,
        [active, back],
        outs,
        [pltpu.VMEM((n, rows, feats), bf16)],
        4 * n * rows * feats * hidden,
    )


def normed(values):
    centered = values - jnp.mean(values, axis=-1, keepdims=True)
    inverse = lax.rsqrt(jnp.mean(centered * centered, axis=-1, keepdims=True) + epsilon)
    return centered * inverse, inverse


def norm_back(grad, scale, unit, inverse):
    g = grad * (1.0 + scale)
    mean_g = jnp.mean(g, axis=-1, keepdims=True)
    mean_gm = jnp.mean(g * unit, axis=-1, keepdims=True)
    return inverse * (g - mean_g - unit * mean_gm)


def exact(onehot, values):
    return jnp.dot(onehot.astype(f32), values, precision=highest)


def fetch_block(layer, params, place):
    _, _, qkv_weight, _, out_weight, _, up_weight, _, down_weight, _ = params
    n, nz, b, z, nh, hd = place
    mine = nh * hd
    shard, feats = out_weight.shape[1:]
    qkv = qkv_weight[layer].reshape(shard, 3, feats)
    qkv = lax.dynamic_slice_in_dim(qkv, b * mine, mine, 2).reshape(shard, 3 * mine)
    hidden = up_weight.shape[2] // (n * nz)
    up = up_weight[layer].reshape(shard, nz, n * hidden)
    up = lax.dynamic_slice_in_dim(up, b * hidden, hidden, 2).reshape(shard, nz * hidden)
    down = lax.dynamic_slice_in_dim(down_weight[layer], b * hidden, hidden, 0)
    start = b * mine
    out = lax.dynamic_slice_in_dim(out_weight[layer], start % shard, mine, 0)
    out = jnp.where(start // shard == z, out, jnp.zeros_like(out))
    return (
        lax.all_gather(qkv, "dp", axis=0, tiled=True),
        lax.psum(out, "dp"),
        lax.all_gather(up, "dp", axis=0, tiled=True),
        lax.all_gather(down, "dp", axis=0, tiled=True),
    )


def per_device(
    tokens,
    cond,
    segments,
    kept,
    cotangent,
    ada_weight,
    ada_bias,
    qkv_weight,
    qv_bias,
    out_weight,
    out_bias,
    up_weight,
    up_bias,
    down_weight,
    down_bias,
):
    params = (
        ada_weight,
        ada_bias,
        qkv_weight,
        qv_bias,
        out_weight,
        out_bias,
        up_weight,
        up_bias,
        down_weight,
        down_bias,
    )
    n, nz = lax.axis_size("blk"), lax.axis_size("dp")
    b, z = lax.axis_index("blk"), lax.axis_index("dp")
    rows, feats = tokens.shape
    keep = kept.shape[0]
    layers = ada_weight.shape[0]
    hd = feats // HEADS
    nh = HEADS // n
    mine = nh * hd
    scale = hd**-0.5
    images = cond.shape[0] // nz
    big = images // 5
    place = (n, nz, b, z, nh, hd)

    lengths = [BIG_LEN] * big + [SMALL_LEN] * (images - big)
    plan, off, base = [], 0, 0
    for length in lengths:
        plan.append((off, length // n, base))
        off += length // n
        base += length
    plan = tuple(plan)
    plan_kept = ((0, keep, 0),)

    silu_c = jax.nn.silu(cond.astype(f32)).astype(bf16)
    shard = ada_weight.shape[1]
    cond_rows = lax.dynamic_slice_in_dim(silu_c, z * shard, shard, 1)
    width = ada_weight.shape[2] // n
    ada_part = lax.dynamic_slice_in_dim(ada_weight, b * width, width, 2)
    partial = jnp.einsum("ik,lkc->lic", cond_rows, ada_part, preferred_element_type=f32)
    held = ada_bias.shape[1]
    bias_part = lax.dynamic_slice_in_dim(ada_bias, (b * width) % held, width, 1).astype(f32)
    partial = partial + jnp.where((b * width) // held == z, bias_part, 0.0)[:, None, :]
    partial = partial.reshape(layers, nz, images, width)
    mod = lax.dynamic_index_in_dim(partial, z, 1, keepdims=False)
    for s in range(1, nz):
        sent = lax.dynamic_index_in_dim(partial, (z + s) % nz, 1, keepdims=False)
        mod = mod + lax.ppermute(sent, "dp", [(i, (i + s) % nz) for i in range(nz)])
    mod = lax.all_gather(mod, "blk", axis=2, tiled=True)

    packed = jnp.concatenate([qv_bias, out_bias, up_bias, down_bias], axis=1)
    packed = lax.all_gather(packed, "dp", axis=0).astype(f32)
    sizes = [a.shape[1] for a in (qv_bias, out_bias, up_bias, down_bias)]
    cuts = [sum(sizes[:i]) for i in range(1, 4)]
    qv_all, out_all, up_all, down_all = jnp.split(packed, cuts, axis=2)
    qv_all = jnp.moveaxis(qv_all, 0, 1).reshape(layers, -1)
    out_all = jnp.moveaxis(out_all, 0, 1).reshape(layers, 1, -1)
    down_all = jnp.moveaxis(down_all, 0, 1).reshape(layers, 1, -1)
    hidden = up_bias.shape[1] // n
    up_mine = lax.dynamic_slice_in_dim(up_all, b * hidden, hidden, 2)
    up_mine = jnp.moveaxis(up_mine, 0, 1).reshape(layers, 1, -1)

    spread = jnp.arange(3 * mine, dtype=jnp.int32)
    spread = spread // hd * PAD + spread % hd
    spread = (spread[:, None] == jnp.arange(3 * nh * PAD, dtype=jnp.int32)[None, :]).astype(bf16)
    spread_out = spread[:mine, : nh * PAD]
    q_bias = lax.dynamic_slice_in_dim(qv_all, b * mine, mine, 1)
    v_bias = lax.dynamic_slice_in_dim(qv_all, feats + b * mine, mine, 1)
    ones = jnp.zeros((1, nh, PAD), f32).at[:, :, PAD_L : PAD_L + 2].set(1.0).reshape(1, nh * PAD)
    place_bias = lambda part: jnp.dot(part, spread_out.astype(f32), precision=highest)
    qkv_bias = jnp.concatenate(
        [
            place_bias(q_bias),
            jnp.zeros((layers, nh * PAD), f32),
            place_bias(v_bias) + ones,
        ],
        axis=1,
    ).reshape(layers, 1, -1)

    local = segments - z * images
    index = jnp.arange(rows, dtype=jnp.int32)
    before = (local[None, :] < local[:, None]) | (
        (local[None, :] == local[:, None]) & (index[None, :] < index[:, None])
    )
    rank = jnp.sum(before.astype(jnp.int32), axis=1)
    order = rank[None, :] == index[:, None]
    chosen = kept[:, None] == index[None, :]
    kept_rank = jnp.sum(jnp.where(chosen, rank[None, :], 0), axis=1)
    kept_local = jnp.sum(jnp.where(chosen, local[None, :], 0), axis=1)
    select = kept_rank[:, None] == index[None, :]
    is_kept = jnp.any(select, axis=0)[:, None]
    tok = jnp.dot(order.astype(bf16), tokens, preferred_element_type=f32)
    cot = jnp.dot(order.astype(bf16), cotangent, preferred_element_type=f32)
    cot_kept = jnp.dot(select.astype(bf16), cot.astype(bf16), preferred_element_type=f32)

    sorted_local = jnp.concatenate(
        [jnp.full((size,), i, jnp.int32) for i, (_, size, _) in enumerate(plan)]
    )
    image_ids = jnp.arange(images, dtype=jnp.int32)
    hot = (sorted_local[:, None] == image_ids[None, :]).astype(f32)
    hot_kept = (kept_local[:, None] == image_ids[None, :]).astype(f32)

    seg_chunks = gather_rows(kept_local, n)
    seg_pieces = {}
    for array, k, first in seg_chunks:
        seg_pieces.setdefault(k, []).append((first, array))
    seg_all = jnp.concatenate(
        [a for k in range(n) for _, a in sorted(seg_pieces[k], key=lambda item: item[0])]
    )
    segs = (seg_all[:, None], seg_all[None, :])

    fetched = [fetch_block(layer, params, place) for layer in range(layers)]

    def forward(layer, x, onehot, images_plan, seg_pair):
        wqkv, wout, wup, wdown = fetched[layer]
        wqkv = dot(wqkv, spread).astype(bf16)
        wout = dot(spread_out, wout, TN).astype(bf16)
        per_row = jnp.dot(onehot, mod[layer], precision=highest)
        shift1, scale1, gate1, shift2, scale2, gate2 = jnp.split(per_row, 6, axis=1)
        unit1, inv1 = normed(x)
        first = (unit1 * (1.0 + scale1) + shift1).astype(bf16)
        first_chunks = gather_rows(first, n)
        qkv, al, mixed, even, odd = attn_forward(
            first_chunks, wqkv, qkv_bias[layer], wout, seg_pair, n, images_plan, scale, nh
        )
        branch = reduce_rows(even, odd, n) + out_all[layer]
        middle = x + gate1 * branch
        unit2, inv2 = normed(middle)
        second = (unit2 * (1.0 + scale2) + shift2).astype(bf16)
        second_chunks = gather_rows(second, n)
        active, slope, even, odd = mlp_forward(second_chunks, wup, up_mine[layer], wdown, n)
        output = reduce_rows(even, odd, n) + down_all[layer]
        stored = (
            (wqkv, wout, wup, wdown),
            (scale1, gate1, scale2, gate2),
            (unit1, inv1, unit2, inv2),
            (first_chunks, second_chunks),
            (qkv, al, mixed, branch, active, slope, output),
        )
        return middle + gate2 * output, stored

    def backward(layer, stored, grad_out, onehot, images_plan, seg_pair):
        (
            (wqkv, wout, wup, wdown),
            (scale1, gate1, scale2, gate2),
            (unit1, inv1, unit2, inv2),
            (first_chunks, second_chunks),
            (qkv, al, mixed, branch, active, slope, output),
        ) = stored
        d_out = (gate2 * grad_out).astype(bf16)
        out_chunks = gather_rows(d_out, n)
        back, even, odd = mlp_backward(out_chunks, wup, wdown, slope)
        g_up, g_down, s_up, s_down = mlp_weights(second_chunks, out_chunks, active, back)
        d_second = reduce_rows(even, odd, n)
        d_middle = grad_out + norm_back(d_second, scale2, unit2, inv2)
        d_branch = (gate1 * d_middle).astype(bf16)
        back_chunks = gather_rows(d_branch, n)
        dqkv, s_qkv, even, odd = attn_backward(
            back_chunks, wqkv, wout, qkv, al, seg_pair, n, images_plan, scale, nh
        )
        g_qkv, g_out, s_out = attn_weights(
            first_chunks, back_chunks, dqkv, mixed, spread, nh, hd
        )
        d_first = reduce_rows(even, odd, n)
        grad_x = d_middle + norm_back(d_first, scale1, unit1, inv1)
        per_row = jnp.concatenate(
            [
                d_first,
                d_first * unit1,
                d_middle * branch,
                d_second,
                d_second * unit2,
                grad_out * output,
            ],
            axis=1,
        )
        grad_mod = jnp.einsum("ri,rm->im", onehot, per_row, precision=highest)
        s_qkv = s_qkv.reshape(3, nh, PAD)[:, :, :hd].reshape(3, mine)
        return grad_x, (g_qkv, g_out, g_up, g_down), (s_qkv, s_out, s_up, s_down, grad_mod)

    def finish(grads, sums):
        g_qkv, g_out, g_up, g_down = grads
        s_qkv, s_out, s_up, s_down, grad_mod = sums
        share = feats // nz
        g_qkv = lax.psum_scatter(g_qkv, "dp", scatter_dimension=0, tiled=True)
        g_up = lax.psum_scatter(g_up, "dp", scatter_dimension=0, tiled=True)
        g_down = lax.psum_scatter(g_down, "dp", scatter_dimension=0, tiled=True)
        g_out = lax.psum(g_out, "dp")
        g_qkv = lax.all_gather(g_qkv, "blk", axis=0).reshape(n, share, 3, mine)
        g_qkv = jnp.transpose(g_qkv, (1, 2, 0, 3)).reshape(share, 3 * feats).astype(f32)
        g_up = lax.all_gather(g_up, "blk", axis=0).reshape(n, share, nz, hidden)
        g_up = jnp.transpose(g_up, (1, 2, 0, 3)).reshape(share, -1).astype(f32)
        g_down = lax.all_gather(g_down, "blk", axis=0, tiled=True).astype(f32)
        g_out = lax.all_gather(g_out, "blk", axis=0, tiled=True)
        g_out = lax.dynamic_slice_in_dim(g_out, z * share, share, 0).astype(f32)
        grad_mod = lax.psum(grad_mod, "blk")
        grad_mod = lax.all_gather(grad_mod, "dp", axis=0, tiled=True)
        g_ada = jnp.dot(cond_rows.astype(f32).T, grad_mod, precision=highest)
        ada_share = ada_bias.shape[1]
        sum_ada = lax.dynamic_slice_in_dim(jnp.sum(grad_mod, axis=0), z * ada_share, ada_share, 0)
        parts = jnp.concatenate([s_up.reshape(-1), s_qkv[0], s_qkv[2]])
        parts = lax.all_gather(parts, "blk", axis=0)
        up_sum = parts[:, : nz * hidden].reshape(n, nz, hidden)
        up_sum = jnp.transpose(up_sum, (1, 0, 2)).reshape(nz, -1)
        q_sum = parts[:, nz * hidden : nz * hidden + mine].reshape(-1)
        v_sum = parts[:, nz * hidden + mine :].reshape(-1)
        qv_sum = jnp.concatenate([q_sum, v_sum]).reshape(nz, -1)
        line = jnp.concatenate(
            [up_sum, qv_sum, s_out.reshape(nz, -1), s_down.reshape(nz, -1)], axis=1
        )
        line = lax.psum(line, "dp")
        line = lax.dynamic_index_in_dim(line, z, 0, keepdims=False)
        widths = [up_sum.shape[1], qv_sum.shape[1], share]
        at = [sum(widths[: i + 1]) for i in range(3)]
        up_line, qv_line, out_line, down_line = jnp.split(line, at)
        return (
            g_ada,
            sum_ada,
            g_qkv,
            qv_line,
            g_out,
            out_line,
            g_up,
            up_line,
            g_down,
            down_line,
        )

    mid, stored0 = forward(0, tok, hot, plan, None)
    mid_kept = exact(select, mid)
    routed, stored1 = forward(1, mid_kept, hot_kept, plan_kept, segs)
    grad_kept, grads1, sums1 = backward(1, stored1, cot_kept, hot_kept, plan_kept, segs)
    out1 = finish(grads1, sums1)
    spread_back = exact(select.T, grad_kept)
    grad_mid = jnp.where(is_kept, spread_back, cot)
    grad_tok, grads0, sums0 = backward(0, stored0, grad_mid, hot, plan, None)
    out0 = finish(grads0, sums0)
    back_order = order.T
    mid_out = exact(back_order, mid)
    final = exact(chosen.T, routed)
    final = jnp.where(jnp.any(chosen, axis=0)[:, None], final, mid_out)
    grad_tokens = exact(back_order, grad_tok)
    stacked = tuple(jnp.stack([a0, a1]) for a0, a1 in zip(out0, out1))
    return (mid_out, final, grad_tokens) + stacked


def solution(mesh):
    return jax.shard_map(
        per_device,
        mesh=mesh,
        in_specs=(
            P(("dp", "blk"), None),
            P(),
            P(("dp", "blk")),
            P(("dp", "blk")),
            P(("dp", "blk"), None),
            P(None, "dp", None),
            P(None, "dp"),
            P(None, "dp", None),
            P(None, "dp"),
            P(None, "dp", None),
            P(None, "dp"),
            P(None, "dp", None),
            P(None, "dp"),
            P(None, "dp", None),
            P(None, "dp"),
        ),
        out_specs=(
            P(("dp", "blk"), None),
            P(("dp", "blk"), None),
            P(("dp", "blk"), None),
            P(None, "dp", None),
            P(None, "dp"),
            P(None, "dp", None),
            P(None, "dp"),
            P(None, "dp", None),
            P(None, "dp"),
            P(None, "dp", None),
            P(None, "dp"),
            P(None, "dp", None),
            P(None, "dp"),
        ),
        check_vma=False,
    )
```
